32 devices in a mesh: fsdp: 8 (over z, x), tp: 4 (over y, core).
Axes of the slice: x: 2, y: 2, z: 4, core: 2. Of those that a mesh axis runs over, the one named last changes fastest.
Arguments:
- activations: bfloat16 [1024, 5120], P('fsdp', 'tp'), may hold values from -6 to 6
- out_grad: bfloat16 [1024, 5120], P('fsdp'), may hold values from -0.25 to 0.25
- momentum: float32 [5120, 5120], P('fsdp', 'tp'), may hold values from -6 to 6
- right_prev: float32 [5120, 256], P('tp'), may hold values from -6 to 6
Outputs:
- new_momentum: float32 [5120, 5120], P('fsdp', 'tp')
- update: float32 [5120, 5120], P('fsdp', 'tp')
- right_next: float32 [5120, 256], P('tp', 'fsdp')
The draws below stay inside these ranges and needn't reach their ends.
All inputs are finite; a program needn't handle non-finite values.
Results may differ from the reference program's by a relative error of at most 0.0003.
Values sent between devices are 32-bit elements; how exact they have to be, the bound alone decides.
A program may use at most 128 MiB of HBM per device.

```python
import math
import jax
import jax.numpy as jnp
from jax import lax

D = 5120
R = 256
TOKENS = 1024


def spiked(drawn, stream_key, source, target, parts, factor):
    def block_of(axis_at):
        return (jnp.arange(drawn.shape[axis_at]) // (drawn.shape[axis_at] // parts)).reshape((-1,) + (1,) * (drawn.ndim - 1 - axis_at))

    first = jax.random.permutation(stream_key, parts)[block_of(target)]
    other_side = (block_of(target) + parts // 2) % parts
    return jnp.where((block_of(source) == first) | (block_of(source) == other_side), factor * drawn, drawn)


def level_of(own_key, extent, cuts, smallest, top_value):
    def one(axis_at, shards_of):
        draws = jax.random.uniform(jax.random.fold_in(jax.random.fold_in(own_key, 6), axis_at), (shards_of,), jnp.float32, smallest / len(cuts), top_value / len(cuts))
        return jnp.repeat(jnp.exp(draws), extent[axis_at] // shards_of).reshape((-1,) + (1,) * (len(extent) - axis_at - 1))

    loudness = one(*cuts[0])
    for cut in cuts[1:]:
        loudness = loudness * one(*cut)
    return loudness


def normal_values(rng, extent, deviation, limit, split=(), dtype=jnp.bfloat16):
    level = level_of(rng, extent, split, -0.22, 0.18) if split else 1.0
    array = jax.random.normal(rng, extent, jnp.float32) * deviation * level
    return jnp.minimum(jnp.maximum(array, -limit), limit).astype(dtype)


def noise_with(rng, shape, deviation, reach, split, heavy, kind=jnp.bfloat16):
    values = deviation * jax.random.normal(rng, shape, jnp.float32)
    if split:
        values = values * level_of(rng, shape, split, -0.22, 0.18)
    return jnp.clip(spiked(values, jax.random.fold_in(rng, 3), *heavy), -reach, reach).astype(kind)


def setup_inputs(seed: int = 0) -> dict:
    key_list = jax.random.split(jax.random.key(seed), 5)
    return {
        "activations": normal_values(key_list[0], (TOKENS, D), 1.0, 6.0, ((0, 8), (1, 4))),
        "out_grad": noise_with(key_list[1], (TOKENS, D), (TOKENS ** -0.5), 0.25, ((0, 8),), (0, 1, 8, 2.0)),
        "momentum": normal_values(key_list[2], (D, D), 1.0, 6.0, ((0, 8), (1, 4)), jnp.float32),
        "right_prev": normal_values(key_list[3], (D, R), 1.0, 6.0, ((0, 4),), jnp.float32),
    }


momentum_decay = 0.95

def reference(activations, out_grad, momentum, right_prev):
    high = lax.Precision.HIGHEST
    grad = lax.dot_general(out_grad.astype(jnp.float32), activations.astype(jnp.float32), (((0,), (0,)), ((), ())), preferred_element_type=jnp.float32)
    buffer = momentum + grad
    left = jnp.dot(buffer, right_prev, precision=high)
    gram = jnp.dot(left.T, left, precision=high)
    lower = jnp.linalg.cholesky(gram)
    basis = lax.linalg.triangular_solve(lower, left, left_side=False, lower=True, transpose_a=True)
    right = jnp.dot(buffer.T, basis, precision=high)
    factor = lax.rsqrt(lax.optimization_barrier(jnp.mean(right * right, axis=0)) + 1e-06)
    right_next = right * factor[None, :]
    new_momentum = buffer - (1.0 - momentum_decay) * jnp.dot(basis, right.T, precision=high)
    update = math.sqrt(D / R) * jnp.dot(basis, right_next.T, precision=high)
    return (new_momentum, update, right_next)
```

```python
import functools
import math

import jax
import jax.numpy as jnp
from jax import lax
from jax.experimental import pallas as pl
from jax.experimental.pallas import tpu as pltpu
from jax.sharding import PartitionSpec as P

HIGH = lax.Precision.HIGHEST
F32 = jnp.float32
BF16 = jnp.bfloat16
LANES = 128
PANEL = 8
VMEM_LIMIT = 56 * 1024 * 1024

momentum_decay = 0.95


def dot(a, b, dims=((1,), (0,))):
    return lax.dot_general(a, b, (dims, ((), ())), precision=HIGH, preferred_element_type=F32)


def remote(src, dst, send, recv, device):
    return pltpu.make_async_remote_copy(
        src_ref=src, dst_ref=dst, send_sem=send, recv_sem=recv,
        device_id=device, device_id_type=pl.DeviceIdType.MESH,
    )


def greet(n, m, f, t):
    barrier = pltpu.get_barrier_semaphore()
    for k in range(1, n):
        pl.semaphore_signal(barrier, inc=1, device_id=(lax.rem(f + k, n), t),
                            device_id_type=pl.DeviceIdType.MESH)
    for k in range(1, m):
        pl.semaphore_signal(barrier, inc=1, device_id=(f, lax.rem(t + k, m)),
                            device_id_type=pl.DeviceIdType.MESH)
    pl.semaphore_wait(barrier, n + m - 2)


def main_kernel(n, m, a_ref, g_ref, mom_ref, p_ref,
                buf_ref, left_ref, gram_ref, s_ref,
                agath, ggath, gsend, gt, lpart, lrecv, gpart, grecv, spart, srecv,
                az_send, az_recv, ax_send, ax_recv, gs_send, gs_recv, gt_send, gt_recv,
                l_send, l_recv, l2_send, l2_recv, q_send, q_recv, q2_send, q2_recv,
                s_send, s_recv, s2_send, s2_recv):
    f = lax.axis_index("fsdp")
    t = lax.axis_index("tp")
    nz = n // 2
    z, x = f // 2, lax.rem(f, 2)
    xpeer = z * 2 + (1 - x)
    tok, wide = a_ref.shape
    quarter = tok // m
    rows = mom_ref.shape[0]
    agath[f] = a_ref[...].astype(F32)
    for d in range(n):
        gsend[d] = g_ref[pl.ds(pl.multiple_of(t * quarter, quarter), quarter),
                         d * rows:(d + 1) * rows].astype(F32)
    ggath[f, t] = gsend[f]
    greet(n, m, f, t)

    for k in range(1, n):
        d = lax.rem(f + k, n)
        remote(gsend.at[d], ggath.at[f, t], gs_send.at[k - 1], gs_recv.at[k - 1], (d, t)).start()

    def az(slot, way, k):
        target = (z + 1) * 2 + x if way == 0 else (z - 1) * 2 + x
        sem = slot // 2
        return remote(agath.at[slot], agath.at[slot], az_send.at[way, k], az_recv.at[sem], (target, t))

    def ax(slot):
        return remote(agath.at[slot], agath.at[slot], ax_send.at[slot // 2], ax_recv.at[slot // 2],
                      (xpeer, t))

    pl.when(z < nz - 1)(lambda: az(f, 0, 0).start())
    pl.when(z > 0)(lambda: az(f, 1, 0).start())
    ax(f).start()

    def gather_step(k):
        @pl.when(z >= k)
        def _():
            slot = f - 2 * k
            az(slot, 0, k).wait_recv()
            pl.when(z < nz - 1)(lambda: az(slot, 0, k).start())
            ax(slot).start()

        @pl.when(z + k < nz)
        def _():
            slot = f + 2 * k
            az(slot, 1, k).wait_recv()
            pl.when(z > 0)(lambda: az(slot, 1, k).start())
            ax(slot).start()

    def gs_wait():
        for k in range(1, n):
            source = lax.rem(f - k + n, n)
            remote(gsend.at[f], ggath.at[source, t], gs_send.at[k - 1], gs_recv.at[k - 1],
                   (source, t)).wait_recv()

    gather_step(1)
    gs_wait()
    for k in range(1, m):
        d = lax.rem(t + k, m)
        remote(ggath.at[:, t], ggath.at[:, t], gt_send.at[k - 1], gt_recv.at[k - 1], (f, d)).start()
    for k in range(2, nz):
        gather_step(k)
    for k in range(1, m):
        source = lax.rem(t - k + m, m)
        remote(ggath.at[:, source], ggath.at[:, source], gt_send.at[k - 1], gt_recv.at[k - 1],
               (f, source)).wait_recv()
    gt[...] = ggath[...].reshape(n * tok, rows).astype(BF16).T
    for zz in range(nz):
        slot = 2 * zz + (1 - x)
        remote(agath.at[slot], agath.at[slot], ax_send.at[zz], ax_recv.at[zz], (xpeer, t)).wait_recv()

    tile = 2 * LANES
    for j in range(wide // tile):
        col = slice(j * tile, (j + 1) * tile)
        part = agath[:, :, col].reshape(n * tok, tile).astype(BF16)
        grad = jnp.dot(gt[...], part, preferred_element_type=F32)
        b = mom_ref[:, col] + grad
        buf_ref[:, col] = b
        term = dot(b, p_ref[col, :])
        lpart[...] = term if j == 0 else lpart[...] + term

    share = rows // m
    for k in range(1, m):
        d = lax.rem(t + k, m)
        remote(lpart.at[pl.ds(pl.multiple_of(d * share, share), share)], lrecv.at[k - 1],
               l_send.at[k - 1], l_recv.at[k - 1], (f, d)).start()
    mine = pl.ds(pl.multiple_of(t * share, share), share)
    for k in range(1, m):
        remote(lpart.at[mine], lrecv.at[k - 1], l_send.at[k - 1], l_recv.at[k - 1], (f, t)).wait_recv()
    total = lpart[mine, :]
    for k in range(1, m):
        total = total + lrecv[k - 1]
    left_ref[mine, :] = total
    for k in range(1, m):
        d = lax.rem(t + k, m)
        remote(left_ref.at[mine], left_ref.at[mine], l2_send.at[k - 1], l2_recv.at[k - 1], (f, d)).start()
    for k in range(1, m):
        source = lax.rem(t - k + m, m)
        theirs = pl.ds(pl.multiple_of(source * share, share), share)
        remote(left_ref.at[theirs], left_ref.at[theirs], l2_send.at[k - 1], l2_recv.at[k - 1],
               (f, source)).wait_recv()

    left = left_ref[...]
    gpart[...] = dot(left, left, ((0,), (0,)))
    gshare = gpart.shape[0] // m
    gmine = pl.ds(pl.multiple_of(t * gshare, gshare), gshare)
    for k in range(1, n):
        d = lax.rem(f + k, n)
        remote(gpart.at[gmine], grecv.at[f], q_send.at[k - 1], q_recv.at[k - 1], (d, t)).start()
    grecv[f] = gpart[gmine, :]

    for j in range(wide // tile):
        col = slice(j * tile, (j + 1) * tile)
        spart[col, :] = dot(buf_ref[:, col], left, ((0,), (0,)))
    sshare = wide // n
    for k in range(1, n):
        d = lax.rem(f + k, n)
        remote(spart.at[pl.ds(pl.multiple_of(d * sshare, sshare), sshare)], srecv.at[k - 1],
               s_send.at[k - 1], s_recv.at[k - 1], (d, t)).start()

    for k in range(1, n):
        source = lax.rem(f - k + n, n)
        remote(gpart.at[gmine], grecv.at[source], q_send.at[k - 1], q_recv.at[k - 1],
               (source, t)).wait_recv()
    gram_ref[gmine, :] = jnp.sum(grecv[...], axis=0)
    for k in range(1, m):
        d = lax.rem(t + k, m)
        remote(gram_ref.at[gmine], gram_ref.at[gmine], q2_send.at[k - 1], q2_recv.at[k - 1],
               (f, d)).start()

    smine = pl.ds(pl.multiple_of(f * sshare, sshare), sshare)
    for k in range(1, n):
        remote(spart.at[smine], srecv.at[k - 1], s_send.at[k - 1], s_recv.at[k - 1],
               (f, t)).wait_recv()
    total = spart[smine, :]
    for k in range(1, n):
        total = total + srecv[k - 1]
    s_ref[smine, :] = total
    for k in range(1, n):
        d = lax.rem(f + k, n)
        remote(s_ref.at[smine], s_ref.at[smine], s2_send.at[k - 1], s2_recv.at[k - 1], (d, t)).start()

    for k in range(1, m):
        source = lax.rem(t - k + m, m)
        theirs = pl.ds(pl.multiple_of(source * gshare, gshare), gshare)
        remote(gram_ref.at[theirs], gram_ref.at[theirs], q2_send.at[k - 1], q2_recv.at[k - 1],
               (f, source)).wait_recv()
    for k in range(1, n):
        source = lax.rem(f - k + n, n)
        theirs = pl.ds(pl.multiple_of(source * sshare, sshare), sshare)
        remote(s_ref.at[theirs], s_ref.at[theirs], s2_send.at[k - 1], s2_recv.at[k - 1],
               (source, t)).wait_recv()

    for k in range(1, n):
        d = lax.rem(f + k, n)
        remote(gsend.at[d], ggath.at[f, t], gs_send.at[k - 1], gs_recv.at[k - 1], (d, t)).wait_send()
        remote(gpart.at[gmine], grecv.at[f], q_send.at[k - 1], q_recv.at[k - 1], (d, t)).wait_send()
        remote(spart.at[pl.ds(pl.multiple_of(d * sshare, sshare), sshare)], srecv.at[k - 1],
               s_send.at[k - 1], s_recv.at[k - 1], (d, t)).wait_send()
        remote(s_ref.at[smine], s_ref.at[smine], s2_send.at[k - 1], s2_recv.at[k - 1], (d, t)).wait_send()
    for k in range(1, m):
        d = lax.rem(t + k, m)
        remote(ggath.at[:, t], ggath.at[:, t], gt_send.at[k - 1], gt_recv.at[k - 1], (f, d)).wait_send()
        remote(lpart.at[pl.ds(pl.multiple_of(d * share, share), share)], lrecv.at[k - 1],
               l_send.at[k - 1], l_recv.at[k - 1], (f, d)).wait_send()
        remote(left_ref.at[mine], left_ref.at[mine], l2_send.at[k - 1], l2_recv.at[k - 1], (f, d)).wait_send()
        remote(gram_ref.at[gmine], gram_ref.at[gmine], q2_send.at[k - 1], q2_recv.at[k - 1],
               (f, d)).wait_send()
    for zz in range(nz):
        ax(2 * zz + x).wait_send()
    for k in range(nz):
        pl.when((z >= k) & (z < nz - 1))(lambda k=k: az(f - 2 * k, 0, k).wait_send())
        pl.when((z + k < nz) & (z > 0))(lambda k=k: az(f + 2 * k, 1, k).wait_send())


def split3(v):
    h = v.astype(BF16)
    r = v - h.astype(F32)
    mid = r.astype(BF16)
    return h.astype(F32), mid.astype(F32), r - mid.astype(F32)


def inverse_factor_kernel(gram_ref, inv_ref, work):
    rank = gram_ref.shape[0]
    work[:, :rank] = gram_ref[...]
    row = lax.broadcasted_iota(jnp.int32, (rank, rank), 0)
    col = lax.broadcasted_iota(jnp.int32, (rank, rank), 1)
    work[:, rank:] = jnp.where(row == col, 1.0, 0.0).astype(F32)
    sub = lax.broadcasted_iota(jnp.int32, (PANEL, 1), 0)
    lane = lax.broadcasted_iota(jnp.int32, (PANEL, rank), 1)

    def step(k, carry):
        start = pl.multiple_of(k * PANEL, PANEL)
        panel = work[pl.ds(start, PANEL), :]
        near = pltpu.roll(panel[:, :rank], lax.rem(rank - start, rank), 1)[:, :LANES]
        pivots = jnp.ones((PANEL, 1), F32)
        for j in range(PANEL):
            column = near[:, j:j + 1]
            pivot = column[j:j + 1, :]
            weight = jnp.where(sub > j, column / pivot, 0.0)
            pivots = jnp.where(sub == j, pivot, pivots)
            near = near - weight * near[j:j + 1, :]
            panel = panel - weight * panel[j:j + 1, :]
        panel = panel * lax.rsqrt(pivots)
        inv_ref[pl.ds(start, PANEL), :] = panel[:, rank:]
        outer = jnp.where(lane >= start + PANEL, panel[:, :rank], 0.0)
        h, mid, low = split3(outer)
        ph, pm, plow = split3(panel)
        lhs = jnp.concatenate([h, h, mid, h, mid, low], axis=0).astype(BF16)
        rhs = jnp.concatenate([ph, pm, ph, plow, pm, ph], axis=0).astype(BF16)
        work[...] = work[...] - lax.dot_general(
            lhs, rhs, (((0,), (0,)), ((), ())), preferred_element_type=F32)
        return carry

    lax.fori_loop(0, rank // PANEL, step, 0)


def factor_kernel(m, size, left_ref, s_ref, inv_ref, basis_ref, right_ref, factor_ref,
                  squares, send, recv):
    f = lax.axis_index("fsdp")
    t = lax.axis_index("tp")
    barrier = pltpu.get_barrier_semaphore()
    for k in range(1, m):
        pl.semaphore_signal(barrier, inc=1, device_id=(f, lax.rem(t + k, m)),
                            device_id_type=pl.DeviceIdType.MESH)
    inv = inv_ref[...]
    right = dot(s_ref[...], inv, ((1,), (1,)))
    right_ref[...] = right
    squares[t] = jnp.broadcast_to(jnp.sum(right * right, axis=0, keepdims=True), squares.shape[1:])
    pl.semaphore_wait(barrier, m - 1)
    copies = [
        remote(squares.at[t], squares.at[t], send.at[k - 1], recv.at[k - 1],
               (f, lax.rem(t + k, m)))
        for k in range(1, m)
    ]
    for copy in copies:
        copy.start()
    basis_ref[...] = dot(left_ref[...], inv, ((1,), (1,)))
    for k in range(1, m):
        source = lax.rem(t - k + m, m)
        remote(squares.at[source], squares.at[source], send.at[k - 1], recv.at[k - 1],
               (f, source)).wait_recv()
    factor_ref[...] = lax.rsqrt(jnp.sum(squares[...], axis=0) / size + 1e-06)
    for copy in copies:
        copy.wait_send()


def output_kernel(scale, buf_ref, basis_ref, right_ref, factor_ref, mom_ref, up_ref, hi, lo):
    @pl.when(pl.program_id(0) == 0)
    def _():
        r = right_ref[...]
        h = r.astype(BF16)
        hi[...] = h
        lo[...] = (r - h.astype(F32)).astype(BF16)

    basis = basis_ref[...]
    both = jnp.concatenate([basis * (momentum_decay - 1.0), basis * (factor_ref[0:1, :] * scale)], axis=0)
    bh = both.astype(BF16)
    bl = (both - bh.astype(F32)).astype(BF16)
    dims = (((1,), (1,)), ((), ()))
    out = lax.dot_general(bh, hi[...], dims, preferred_element_type=F32)
    out += lax.dot_general(bl, hi[...], dims, preferred_element_type=F32)
    out += lax.dot_general(bh, lo[...], dims, preferred_element_type=F32)
    tall = basis.shape[0]
    mom_ref[...] = buf_ref[...] + out[:tall]
    up_ref[...] = out[tall:]


def sds(*shape):
    return jax.ShapeDtypeStruct(shape, F32)


def kernels_on_device(n, m, activations, out_grad, momentum, right_prev):
    tok, wide = activations.shape
    rows = momentum.shape[0]
    rank = right_prev.shape[1]
    vm = pl.BlockSpec(memory_space=pltpu.VMEM)
    dma = pltpu.SemaphoreType.DMA
    full = rows * n
    nz = n // 2
    buffer, left, gram, s = pl.pallas_call(
        functools.partial(main_kernel, n, m),
        out_shape=(sds(rows, wide), sds(rows, rank), sds(rank, rank), sds(wide, rank)),
        in_specs=[vm] * 4,
        out_specs=(vm,) * 4,
        scratch_shapes=[
            pltpu.VMEM((n, tok, wide), F32),
            pltpu.VMEM((n, m, tok // m, rows), F32),
            pltpu.VMEM((n, tok // m, rows), F32),
            pltpu.VMEM((rows, n * tok), BF16),
            pltpu.VMEM((rows, rank), F32),
            pltpu.VMEM((m - 1, rows // m, rank), F32),
            pltpu.VMEM((rank, rank), F32),
            pltpu.VMEM((n, rank // m, rank), F32),
            pltpu.VMEM((wide, rank), F32),
            pltpu.VMEM((n - 1, wide // n, rank), F32),
            dma((2, nz)), dma((nz,)), dma((nz,)), dma((nz,)),
            dma((n - 1,)), dma((n - 1,)), dma((m - 1,)), dma((m - 1,)),
            dma((m - 1,)), dma((m - 1,)), dma((m - 1,)), dma((m - 1,)),
            dma((n - 1,)), dma((n - 1,)), dma((m - 1,)), dma((m - 1,)),
            dma((n - 1,)), dma((n - 1,)), dma((n - 1,)), dma((n - 1,)),
        ],
        compiler_params=pltpu.CompilerParams(
            collective_id=0, has_side_effects=True, vmem_limit_bytes=VMEM_LIMIT),
    )(activations, out_grad, momentum, right_prev)
    inverse = pl.pallas_call(
        inverse_factor_kernel,
        out_shape=sds(rank, rank),
        in_specs=[vm],
        out_specs=vm,
        scratch_shapes=[pltpu.VMEM((rank, 2 * rank), F32)],
    )(gram)
    basis, right, factor = pl.pallas_call(
        functools.partial(factor_kernel, m, full),
        out_shape=(sds(rows, rank), sds(wide, rank), sds(8, rank)),
        in_specs=[vm] * 3,
        out_specs=(vm,) * 3,
        scratch_shapes=[pltpu.VMEM((m, 8, rank), F32), dma((m - 1,)), dma((m - 1,))],
        compiler_params=pltpu.CompilerParams(
            collective_id=1, has_side_effects=True, vmem_limit_bytes=VMEM_LIMIT),
    )(left, s, inverse)
    tall = LANES
    size = wide * m
    new_momentum, update = pl.pallas_call(
        functools.partial(output_kernel, math.sqrt(size / rank)),
        grid=(rows // tall,),
        out_shape=(sds(rows, wide), sds(rows, wide)),
        in_specs=[
            pl.BlockSpec((tall, wide), lambda i: (i, 0)),
            pl.BlockSpec((tall, rank), lambda i: (i, 0)),
            pl.BlockSpec((wide, rank), lambda i: (0, 0)),
            pl.BlockSpec((8, rank), lambda i: (0, 0)),
        ],
        out_specs=(
            pl.BlockSpec((tall, wide), lambda i: (i, 0)),
            pl.BlockSpec((tall, wide), lambda i: (i, 0)),
        ),
        scratch_shapes=[pltpu.VMEM((wide, rank), BF16)] * 2,
        compiler_params=pltpu.CompilerParams(vmem_limit_bytes=VMEM_LIMIT),
    )(buffer, basis, right, factor)
    own = rank // n
    first = lax.axis_index("fsdp") * own
    right_owned = lax.dynamic_slice_in_dim(right, first, own, 1) * lax.dynamic_slice_in_dim(
        factor[0:1], first, own, 1)
    return new_momentum, update, right_owned


def plain_on_device(activations, out_grad, momentum, right_prev):
    size = momentum.shape[1] * lax.axis_size("tp")
    rank = right_prev.shape[1]
    grad = lax.psum_scatter(
        lax.dot_general(out_grad, activations, (((0,), (0,)), ((), ())), preferred_element_type=F32),
        "fsdp", scatter_dimension=0, tiled=True)
    buffer = momentum + grad
    left = lax.psum(dot(buffer, right_prev), "tp")
    gram = lax.psum(dot(left.T, left), "fsdp")
    lower = jnp.linalg.cholesky(gram)
    basis = lax.linalg.triangular_solve(lower, left, left_side=False, lower=True, transpose_a=True)
    right = lax.psum(dot(buffer.T, basis), "fsdp")
    squares = lax.psum(jnp.sum(right * right, axis=0), "tp")
    factor = lax.rsqrt(squares / size + 1e-06)
    right_next = right * factor[None, :]
    new_momentum = buffer - (1.0 - momentum_decay) * dot(basis, right.T)
    update = math.sqrt(size / rank) * dot(basis, right_next.T)
    own = rank // lax.axis_size("fsdp")
    right_owned = lax.dynamic_slice_in_dim(right_next, lax.axis_index("fsdp") * own, own, 1)
    return new_momentum, update, right_owned


def solution(mesh):
    n, m = mesh.shape["fsdp"], mesh.shape["tp"]

    def on_device(activations, out_grad, momentum, right_prev):
        tok, wide = activations.shape
        rows = momentum.shape[0]
        if rows % LANES == 0 and wide % (2 * LANES) == 0 and 4 * n * tok * (wide + rows) <= VMEM_LIMIT // 4:
            return kernels_on_device(n, m, activations, out_grad, momentum, right_prev)
        return plain_on_device(activations, out_grad, momentum, right_prev)

    return jax.shard_map(
        on_device,
        mesh=mesh,
        in_specs=(P("fsdp", "tp"), P("fsdp", None), P("fsdp", "tp"), P("tp", None)),
        out_specs=(P("fsdp", "tp"), P("fsdp", "tp"), P("tp", "fsdp")),
        check_vma=False,
    )
```

```python
import functools
import math

import jax
import jax.numpy as jnp
from jax import lax
from jax.experimental import pallas as pl
from jax.experimental.pallas import tpu as pltpu
from jax.sharding import PartitionSpec as P

HIGH = lax.Precision.HIGHEST
F32 = jnp.float32
BF16 = jnp.bfloat16
LANES = 128
PANEL = 8
VMEM_LIMIT = 56 * 1024 * 1024

momentum_decay = 0.95


def dot(a, b, dims=((1,), (0,))):
    return lax.dot_general(a, b, (dims, ((), ())), precision=HIGH, preferred_element_type=F32)


def remote(src, dst, send, recv, device):
    return pltpu.make_async_remote_copy(
        src_ref=src, dst_ref=dst, send_sem=send, recv_sem=recv,
        device_id=device, device_id_type=pl.DeviceIdType.MESH,
    )


def greet(n, m, f, t):
    barrier = pltpu.get_barrier_semaphore()
    for k in range(1, n):
        pl.semaphore_signal(barrier, inc=1, device_id=(lax.rem(f + k, n), t),
                            device_id_type=pl.DeviceIdType.MESH)
    for k in range(1, m):
        pl.semaphore_signal(barrier, inc=1, device_id=(f, lax.rem(t + k, m)),
                            device_id_type=pl.DeviceIdType.MESH)
    pl.semaphore_wait(barrier, n + m - 2)


def main_kernel(n, m, a_ref, g_ref, mom_ref, p_ref,
                buf_ref, basis_ref, right_ref, factor_ref,
                left_ref, gram_ref, s_ref, inv_ref, work, squares, c_send, c_recv,
                agath, ggath, gsend, gt, lpart, lrecv, gpart, grecv, spart, srecv,
                az_send, az_recv, ax_send, ax_recv, gs_send, gs_recv, gt_send, gt_recv,
                l_send, l_recv, l2_send, l2_recv, q_send, q_recv, q2_send, q2_recv,
                s_send, s_recv, s2_send, s2_recv):
    f = lax.axis_index("fsdp")
    t = lax.axis_index("tp")
    nz = n // 2
    z, x = f // 2, lax.rem(f, 2)
    xpeer = z * 2 + (1 - x)
    tok, wide = a_ref.shape
    quarter = tok // m
    rows = mom_ref.shape[0]
    agath[f] = a_ref[...].astype(F32)
    for d in range(n):
        gsend[d] = g_ref[pl.ds(pl.multiple_of(t * quarter, quarter), quarter),
                         d * rows:(d + 1) * rows].astype(F32)
    ggath[f, t] = gsend[f]
    greet(n, m, f, t)

    for k in range(1, n):
        d = lax.rem(f + k, n)
        remote(gsend.at[d], ggath.at[f, t], gs_send.at[k - 1], gs_recv.at[k - 1], (d, t)).start()

    def az(slot, way, k):
        target = (z + 1) * 2 + x if way == 0 else (z - 1) * 2 + x
        sem = slot // 2
        return remote(agath.at[slot], agath.at[slot], az_send.at[way, k], az_recv.at[sem], (target, t))

    def ax(slot):
        return remote(agath.at[slot], agath.at[slot], ax_send.at[slot // 2], ax_recv.at[slot // 2],
                      (xpeer, t))

    pl.when(z < nz - 1)(lambda: az(f, 0, 0).start())
    pl.when(z > 0)(lambda: az(f, 1, 0).start())
    ax(f).start()

    def gather_step(k):
        @pl.when(z >= k)
        def _():
            slot = f - 2 * k
            az(slot, 0, k).wait_recv()
            pl.when(z < nz - 1)(lambda: az(slot, 0, k).start())
            ax(slot).start()

        @pl.when(z + k < nz)
        def _():
            slot = f + 2 * k
            az(slot, 1, k).wait_recv()
            pl.when(z > 0)(lambda: az(slot, 1, k).start())
            ax(slot).start()

    def gs_wait():
        for k in range(1, n):
            source = lax.rem(f - k + n, n)
            remote(gsend.at[f], ggath.at[source, t], gs_send.at[k - 1], gs_recv.at[k - 1],
                   (source, t)).wait_recv()

    gather_step(1)
    gs_wait()
    for k in range(1, m):
        d = lax.rem(t + k, m)
        remote(ggath.at[:, t], ggath.at[:, t], gt_send.at[k - 1], gt_recv.at[k - 1], (f, d)).start()
    for k in range(2, nz):
        gather_step(k)
    for k in range(1, m):
        source = lax.rem(t - k + m, m)
        remote(ggath.at[:, source], ggath.at[:, source], gt_send.at[k - 1], gt_recv.at[k - 1],
               (f, source)).wait_recv()
    gt[...] = ggath[...].reshape(n * tok, rows).astype(BF16).T
    for zz in range(nz):
        slot = 2 * zz + (1 - x)
        remote(agath.at[slot], agath.at[slot], ax_send.at[zz], ax_recv.at[zz], (xpeer, t)).wait_recv()

    tile = 2 * LANES
    for j in range(wide // tile):
        col = slice(j * tile, (j + 1) * tile)
        part = agath[:, :, col].reshape(n * tok, tile).astype(BF16)
        grad = jnp.dot(gt[...], part, preferred_element_type=F32)
        b = mom_ref[:, col] + grad
        buf_ref[:, col] = b
        term = dot(b, p_ref[col, :])
        lpart[...] = term if j == 0 else lpart[...] + term

    share = rows // m
    for k in range(1, m):
        d = lax.rem(t + k, m)
        remote(lpart.at[pl.ds(pl.multiple_of(d * share, share), share)], lrecv.at[k - 1],
               l_send.at[k - 1], l_recv.at[k - 1], (f, d)).start()
    mine = pl.ds(pl.multiple_of(t * share, share), share)
    for k in range(1, m):
        remote(lpart.at[mine], lrecv.at[k - 1], l_send.at[k - 1], l_recv.at[k - 1], (f, t)).wait_recv()
    total = lpart[mine, :]
    for k in range(1, m):
        total = total + lrecv[k - 1]
    left_ref[mine, :] = total
    for k in range(1, m):
        d = lax.rem(t + k, m)
        remote(left_ref.at[mine], left_ref.at[mine], l2_send.at[k - 1], l2_recv.at[k - 1], (f, d)).start()
    for k in range(1, m):
        source = lax.rem(t - k + m, m)
        theirs = pl.ds(pl.multiple_of(source * share, share), share)
        remote(left_ref.at[theirs], left_ref.at[theirs], l2_send.at[k - 1], l2_recv.at[k - 1],
               (f, source)).wait_recv()

    left = left_ref[...]
    gpart[...] = dot(left, left, ((0,), (0,)))
    gshare = gpart.shape[0] // m
    gmine = pl.ds(pl.multiple_of(t * gshare, gshare), gshare)
    for k in range(1, n):
        d = lax.rem(f + k, n)
        remote(gpart.at[gmine], grecv.at[f], q_send.at[k - 1], q_recv.at[k - 1], (d, t)).start()
    grecv[f] = gpart[gmine, :]

    for j in range(wide // tile):
        col = slice(j * tile, (j + 1) * tile)
        spart[col, :] = dot(buf_ref[:, col], left, ((0,), (0,)))
    sshare = wide // n
    for k in range(1, n):
        d = lax.rem(f + k, n)
        remote(spart.at[pl.ds(pl.multiple_of(d * sshare, sshare), sshare)], srecv.at[k - 1],
               s_send.at[k - 1], s_recv.at[k - 1], (d, t)).start()

    for k in range(1, n):
        source = lax.rem(f - k + n, n)
        remote(gpart.at[gmine], grecv.at[source], q_send.at[k - 1], q_recv.at[k - 1],
               (source, t)).wait_recv()
    gram_ref[gmine, :] = jnp.sum(grecv[...], axis=0)
    for k in range(1, m):
        d = lax.rem(t + k, m)
        remote(gram_ref.at[gmine], gram_ref.at[gmine], q2_send.at[k - 1], q2_recv.at[k - 1],
               (f, d)).start()

    for k in range(1, m):
        source = lax.rem(t - k + m, m)
        theirs = pl.ds(pl.multiple_of(source * gshare, gshare), gshare)
        remote(gram_ref.at[theirs], gram_ref.at[theirs], q2_send.at[k - 1], q2_recv.at[k - 1],
               (f, source)).wait_recv()
    inv_ref[...] = jnp.zeros_like(inv_ref)
    inverse_begin(gram_ref, work)
    inverse_rows(work, inv_ref, 0, gram_ref.shape[0] // 2)
    smine = pl.ds(pl.multiple_of(f * sshare, sshare), sshare)
    for k in range(1, n):
        remote(spart.at[smine], srecv.at[k - 1], s_send.at[k - 1], s_recv.at[k - 1],
               (f, t)).wait_recv()
    total = spart[smine, :]
    for k in range(1, n):
        total = total + srecv[k - 1]
    s_ref[smine, :] = total
    for k in range(1, n):
        d = lax.rem(f + k, n)
        remote(s_ref.at[smine], s_ref.at[smine], s2_send.at[k - 1], s2_recv.at[k - 1], (d, t)).start()

    inverse_rows(work, inv_ref, gram_ref.shape[0] // 2, gram_ref.shape[0])
    inv = inv_ref[...]
    for k in range(1, n):
        source = lax.rem(f - k + n, n)
        theirs = pl.ds(pl.multiple_of(source * sshare, sshare), sshare)
        remote(s_ref.at[theirs], s_ref.at[theirs], s2_send.at[k - 1], s2_recv.at[k - 1],
               (source, t)).wait_recv()

    right = dot(s_ref[...], inv, ((1,), (1,)))
    right_ref[...] = right
    squares[t] = jnp.broadcast_to(jnp.sum(right * right, axis=0, keepdims=True), squares.shape[1:])
    for k in range(1, m):
        remote(squares.at[t], squares.at[t], c_send.at[k - 1], c_recv.at[k - 1],
               (f, lax.rem(t + k, m))).start()
    basis_ref[...] = dot(left_ref[...], inv, ((1,), (1,)))
    for k in range(1, m):
        source = lax.rem(t - k + m, m)
        remote(squares.at[source], squares.at[source], c_send.at[k - 1], c_recv.at[k - 1],
               (f, source)).wait_recv()
    factor_ref[...] = lax.rsqrt(jnp.sum(squares[...], axis=0) / (rows * n) + 1e-06)

    for k in range(1, n):
        d = lax.rem(f + k, n)
        remote(gsend.at[d], ggath.at[f, t], gs_send.at[k - 1], gs_recv.at[k - 1], (d, t)).wait_send()
        remote(gpart.at[gmine], grecv.at[f], q_send.at[k - 1], q_recv.at[k - 1], (d, t)).wait_send()
        remote(spart.at[pl.ds(pl.multiple_of(d * sshare, sshare), sshare)], srecv.at[k - 1],
               s_send.at[k - 1], s_recv.at[k - 1], (d, t)).wait_send()
        remote(s_ref.at[smine], s_ref.at[smine], s2_send.at[k - 1], s2_recv.at[k - 1], (d, t)).wait_send()
    for k in range(1, m):
        d = lax.rem(t + k, m)
        remote(ggath.at[:, t], ggath.at[:, t], gt_send.at[k - 1], gt_recv.at[k - 1], (f, d)).wait_send()
        remote(lpart.at[pl.ds(pl.multiple_of(d * share, share), share)], lrecv.at[k - 1],
               l_send.at[k - 1], l_recv.at[k - 1], (f, d)).wait_send()
        remote(left_ref.at[mine], left_ref.at[mine], l2_send.at[k - 1], l2_recv.at[k - 1], (f, d)).wait_send()
        remote(gram_ref.at[gmine], gram_ref.at[gmine], q2_send.at[k - 1], q2_recv.at[k - 1],
               (f, d)).wait_send()
        remote(squares.at[t], squares.at[t], c_send.at[k - 1], c_recv.at[k - 1], (f, d)).wait_send()
    for zz in range(nz):
        ax(2 * zz + x).wait_send()
    for k in range(nz):
        pl.when((z >= k) & (z < nz - 1))(lambda k=k: az(f - 2 * k, 0, k).wait_send())
        pl.when((z + k < nz) & (z > 0))(lambda k=k: az(f + 2 * k, 1, k).wait_send())


def split3(v):
    h = v.astype(BF16)
    r = v - h.astype(F32)
    mid = r.astype(BF16)
    return h.astype(F32), mid.astype(F32), r - mid.astype(F32)


def inverse_begin(gram_ref, work):
    rank = gram_ref.shape[0]
    work[:, :rank] = gram_ref[...]
    row = lax.broadcasted_iota(jnp.int32, (rank, rank), 0)
    col = lax.broadcasted_iota(jnp.int32, (rank, rank), 1)
    work[:, rank:] = jnp.where(row == col, 1.0, 0.0).astype(F32)


def inverse_rows(work, inv_ref, first, last):
    rank = work.shape[0]
    some = LANES // 2
    sub = lax.broadcasted_iota(jnp.int32, (PANEL, 1), 0)
    for top in range(first, last, some):
        base = top // LANES * LANES
        end = rank + base + LANES
        lane = lax.broadcasted_iota(jnp.int32, (PANEL, rank - base), 1) + base

        def step(k, carry):
            start = pl.multiple_of(top + k * PANEL, PANEL)
            panel = work[pl.ds(start, PANEL), base:end]
            near = pltpu.roll(panel[:, :LANES], lax.rem(base + LANES - start, LANES), 1)
            pivots = jnp.ones((PANEL, 1), F32)
            for j in range(PANEL):
                column = near[:, j:j + 1]
                pivot = column[j:j + 1, :]
                weight = jnp.where(sub > j, column / pivot, 0.0)
                pivots = jnp.where(sub == j, pivot, pivots)
                near = near - weight * near[j:j + 1, :]
                panel = panel - weight * panel[j:j + 1, :]
            panel = panel * lax.rsqrt(pivots)
            inv_ref[pl.ds(start, PANEL), :base + LANES] = panel[:, rank - base:]
            outer = jnp.where(lane >= start + PANEL, panel[:, :rank - base], 0.0)[:, top - base:]
            h, mid, low = split3(outer)
            ph, pm, plow = split3(panel)
            lhs = jnp.concatenate([h, h, mid, h, mid, low], axis=0).astype(BF16)
            rhs = jnp.concatenate([ph, pm, ph, plow, pm, ph], axis=0).astype(BF16)
            work[top:, base:end] = work[top:, base:end] - lax.dot_general(
                lhs, rhs, (((0,), (0,)), ((), ())), preferred_element_type=F32)
            return carry

        lax.fori_loop(0, some // PANEL, step, 0)


def output_kernel(scale, buf_ref, basis_ref, right_ref, factor_ref, mom_ref, up_ref, hi, lo):
    @pl.when(pl.program_id(0) == 0)
    def _():
        r = right_ref[...]
        h = r.astype(BF16)
        hi[...] = h
        lo[...] = (r - h.astype(F32)).astype(BF16)

    basis = basis_ref[...]
    both = jnp.concatenate([basis * (momentum_decay - 1.0), basis * (factor_ref[0:1, :] * scale)], axis=0)
    bh = both.astype(BF16)
    bl = (both - bh.astype(F32)).astype(BF16)
    dims = (((1,), (1,)), ((), ()))
    out = lax.dot_general(bh, hi[...], dims, preferred_element_type=F32)
    out += lax.dot_general(bl, hi[...], dims, preferred_element_type=F32)
    out += lax.dot_general(bh, lo[...], dims, preferred_element_type=F32)
    tall = basis.shape[0]
    mom_ref[...] = buf_ref[...] + out[:tall]
    up_ref[...] = out[tall:]


def sds(*shape):
    return jax.ShapeDtypeStruct(shape, F32)


def kernels_on_device(n, m, activations, out_grad, momentum, right_prev):
    tok, wide = activations.shape
    rows = momentum.shape[0]
    rank = right_prev.shape[1]
    vm = pl.BlockSpec(memory_space=pltpu.VMEM)
    dma = pltpu.SemaphoreType.DMA
    nz = n // 2
    buffer, basis, right, factor = pl.pallas_call(
        functools.partial(main_kernel, n, m),
        out_shape=(sds(rows, wide), sds(rows, rank), sds(wide, rank), sds(8, rank)),
        in_specs=[vm] * 4,
        out_specs=(vm,) * 4,
        scratch_shapes=[
            pltpu.VMEM((rows, rank), F32),
            pltpu.VMEM((rank, rank), F32),
            pltpu.VMEM((wide, rank), F32),
            pltpu.VMEM((rank, rank), F32),
            pltpu.VMEM((rank, 2 * rank), F32),
            pltpu.VMEM((m, 8, rank), F32),
            dma((m - 1,)), dma((m - 1,)),
            pltpu.VMEM((n, tok, wide), F32),
            pltpu.VMEM((n, m, tok // m, rows), F32),
            pltpu.VMEM((n, tok // m, rows), F32),
            pltpu.VMEM((rows, n * tok), BF16),
            pltpu.VMEM((rows, rank), F32),
            pltpu.VMEM((m - 1, rows // m, rank), F32),
            pltpu.VMEM((rank, rank), F32),
            pltpu.VMEM((n, rank // m, rank), F32),
            pltpu.VMEM((wide, rank), F32),
            pltpu.VMEM((n - 1, wide // n, rank), F32),
            dma((2, nz)), dma((nz,)), dma((nz,)), dma((nz,)),
            dma((n - 1,)), dma((n - 1,)), dma((m - 1,)), dma((m - 1,)),
            dma((m - 1,)), dma((m - 1,)), dma((m - 1,)), dma((m - 1,)),
            dma((n - 1,)), dma((n - 1,)), dma((m - 1,)), dma((m - 1,)),
            dma((n - 1,)), dma((n - 1,)), dma((n - 1,)), dma((n - 1,)),
        ],
        compiler_params=pltpu.CompilerParams(
            collective_id=0, has_side_effects=True, vmem_limit_bytes=VMEM_LIMIT),
    )(activations, out_grad, momentum, right_prev)
    tall = LANES
    size = wide * m
    new_momentum, update = pl.pallas_call(
        functools.partial(output_kernel, math.sqrt(size / rank)),
        grid=(rows // tall,),
        out_shape=(sds(rows, wide), sds(rows, wide)),
        in_specs=[
            pl.BlockSpec((tall, wide), lambda i: (i, 0)),
            pl.BlockSpec((tall, rank), lambda i: (i, 0)),
            pl.BlockSpec((wide, rank), lambda i: (0, 0)),
            pl.BlockSpec((8, rank), lambda i: (0, 0)),
        ],
        out_specs=(
            pl.BlockSpec((tall, wide), lambda i: (i, 0)),
            pl.BlockSpec((tall, wide), lambda i: (i, 0)),
        ),
        scratch_shapes=[pltpu.VMEM((wide, rank), BF16)] * 2,
        compiler_params=pltpu.CompilerParams(vmem_limit_bytes=VMEM_LIMIT),
    )(buffer, basis, right, factor)
    own = rank // n
    first = lax.axis_index("fsdp") * own
    right_owned = lax.dynamic_slice_in_dim(right, first, own, 1) * lax.dynamic_slice_in_dim(
        factor[0:1], first, own, 1)
    return new_momentum, update, right_owned


def plain_on_device(activations, out_grad, momentum, right_prev):
    size = momentum.shape[1] * lax.axis_size("tp")
    rank = right_prev.shape[1]
    grad = lax.psum_scatter(
        lax.dot_general(out_grad, activations, (((0,), (0,)), ((), ())), preferred_element_type=F32),
        "fsdp", scatter_dimension=0, tiled=True)
    buffer = momentum + grad
    left = lax.psum(dot(buffer, right_prev), "tp")
    gram = lax.psum(dot(left.T, left), "fsdp")
    lower = jnp.linalg.cholesky(gram)
    basis = lax.linalg.triangular_solve(lower, left, left_side=False, lower=True, transpose_a=True)
    right = lax.psum(dot(buffer.T, basis), "fsdp")
    squares = lax.psum(jnp.sum(right * right, axis=0), "tp")
    factor = lax.rsqrt(squares / size + 1e-06)
    right_next = right * factor[None, :]
    new_momentum = buffer - (1.0 - momentum_decay) * dot(basis, right.T)
    update = math.sqrt(size / rank) * dot(basis, right_next.T)
    own = rank // lax.axis_size("fsdp")
    right_owned = lax.dynamic_slice_in_dim(right_next, lax.axis_index("fsdp") * own, own, 1)
    return new_momentum, update, right_owned


def solution(mesh):
    n, m = mesh.shape["fsdp"], mesh.shape["tp"]

    def on_device(activations, out_grad, momentum, right_prev):
        tok, wide = activations.shape
        rows = momentum.shape[0]
        if rows % LANES == 0 and wide % (2 * LANES) == 0 and 4 * n * tok * (wide + rows) <= VMEM_LIMIT // 4:
            return kernels_on_device(n, m, activations, out_grad, momentum, right_prev)
        return plain_on_device(activations, out_grad, momentum, right_prev)

    return jax.shard_map(
        on_device,
        mesh=mesh,
        in_specs=(P("fsdp", "tp"), P("fsdp", None), P("fsdp", "tp"), P("tp", None)),
        out_specs=(P("fsdp", "tp"), P("fsdp", "tp"), P("tp", "fsdp")),
        check_vma=False,
    )
```

```python
import functools
import math

import jax
import jax.numpy as jnp
from jax import lax
from jax.experimental import pallas as pl
from jax.experimental.pallas import tpu as pltpu
from jax.sharding import PartitionSpec as P

HIGH = lax.Precision.HIGHEST
F32 = jnp.float32
BF16 = jnp.bfloat16
LANES = 128
PANEL = 8
CHUNKS = 4
VMEM_LIMIT = 56 * 1024 * 1024

momentum_decay = 0.95


def dot(a, b, dims=((1,), (0,))):
    return lax.dot_general(a, b, (dims, ((), ())), precision=HIGH, preferred_element_type=F32)


def remote(src, dst, send, recv, device):
    return pltpu.make_async_remote_copy(
        src_ref=src, dst_ref=dst, send_sem=send, recv_sem=recv,
        device_id=device, device_id_type=pl.DeviceIdType.MESH,
    )


def greet(n, m, f, t):
    barrier = pltpu.get_barrier_semaphore()
    for k in range(1, n):
        pl.semaphore_signal(barrier, inc=1, device_id=(lax.rem(f + k, n), t),
                            device_id_type=pl.DeviceIdType.MESH)
    for k in range(1, m):
        pl.semaphore_signal(barrier, inc=1, device_id=(f, lax.rem(t + k, m)),
                            device_id_type=pl.DeviceIdType.MESH)
    pl.semaphore_wait(barrier, n + m - 2)


def main_kernel(n, m, a_ref, g_ref, mom_ref, p_hbm,
                buf_out, basis_ref, right_ref, factor_ref,
                buf_ref, p_ref, own_sem, left_ref, gram_ref, s_ref, inv_ref, work, squares, c_send, c_recv,
                agath, ggath, gsend, gt, lpart, lrecv, gpart, grecv, spart, srecv,
                az_send, az_recv, ax_send, ax_recv, gs_send, gs_recv, gt_send, gt_recv,
                l_send, l_recv, l2_send, l2_recv, q_send, q_recv, q2_send, q2_recv,
                s_send, s_recv, s2_send, s2_recv):
    f = lax.axis_index("fsdp")
    t = lax.axis_index("tp")
    nz = n // 2
    z, x = f // 2, lax.rem(f, 2)
    xpeer = z * 2 + (1 - x)
    tok, wide = a_ref.shape
    quarter = tok // m
    rows = mom_ref.shape[0]
    load_momentum = pltpu.make_async_copy(mom_ref, buf_ref, own_sem.at[0])
    load_right = pltpu.make_async_copy(p_hbm, p_ref, own_sem.at[1])
    store_buffer = pltpu.make_async_copy(buf_ref, buf_out, own_sem.at[2])
    load_momentum.start()
    load_right.start()
    agath[f] = a_ref[...].astype(F32).reshape(agath.shape[1:])
    for d in range(n):
        gsend[d] = g_ref[pl.ds(pl.multiple_of(t * quarter, quarter), quarter),
                         d * rows:(d + 1) * rows].astype(F32)
    ggath[f, t] = gsend[f]
    greet(n, m, f, t)

    for k in range(1, n):
        d = lax.rem(f + k, n)
        remote(gsend.at[d], ggath.at[f, t], gs_send.at[k - 1], gs_recv.at[k - 1], (d, t)).start()

    def az(slot, c, way, k):
        target = (z + 1) * 2 + x if way == 0 else (z - 1) * 2 + x
        return remote(agath.at[slot, c], agath.at[slot, c], az_send.at[way, k, c],
                      az_recv.at[slot // 2, c], (target, t))

    def ax(slot, c):
        return remote(agath.at[slot, c], agath.at[slot, c], ax_send.at[slot // 2, c],
                      ax_recv.at[slot // 2, c], (xpeer, t))

    for c in range(CHUNKS):
        pl.when(z < nz - 1)(lambda c=c: az(f, c, 0, 0).start())
        pl.when(z > 0)(lambda c=c: az(f, c, 1, 0).start())
        ax(f, c).start()

    def gather_step(k):
        for c in range(CHUNKS):
            @pl.when(z >= k)
            def _():
                slot = f - 2 * k
                az(slot, c, 0, k).wait_recv()
                pl.when(z < nz - 1)(lambda: az(slot, c, 0, k).start())
                ax(slot, c).start()

            @pl.when(z + k < nz)
            def _():
                slot = f + 2 * k
                az(slot, c, 1, k).wait_recv()
                pl.when(z > 0)(lambda: az(slot, c, 1, k).start())
                ax(slot, c).start()

    def gs_wait():
        for k in range(1, n):
            source = lax.rem(f - k + n, n)
            remote(gsend.at[f], ggath.at[source, t], gs_send.at[k - 1], gs_recv.at[k - 1],
                   (source, t)).wait_recv()

    gather_step(1)
    gs_wait()
    for k in range(1, m):
        d = lax.rem(t + k, m)
        remote(ggath.at[:, t], ggath.at[:, t], gt_send.at[k - 1], gt_recv.at[k - 1], (f, d)).start()
    for k in range(2, nz):
        gather_step(k)
    for k in range(1, m):
        source = lax.rem(t - k + m, m)
        remote(ggath.at[:, source], ggath.at[:, source], gt_send.at[k - 1], gt_recv.at[k - 1],
               (f, source)).wait_recv()
    gt[...] = ggath[...].reshape(n * tok, rows).astype(BF16).T
    for zz in range(nz):
        for c in range(CHUNKS):
            ax(2 * zz + (1 - x), c).wait_recv()

    load_momentum.wait()
    load_right.wait()
    tile = 2 * LANES
    for j in range(wide // tile):
        col = slice(j * tile, (j + 1) * tile)
        part = agath[:, :, :, col].reshape(n * tok, tile).astype(BF16)
        grad = jnp.dot(gt[...], part, preferred_element_type=F32)
        b = buf_ref[:, col] + grad
        buf_ref[:, col] = b
        term = dot(b, p_ref[col, :])
        lpart[...] = term if j == 0 else lpart[...] + term

    store_buffer.start()

    share = rows // m
    for k in range(1, m):
        d = lax.rem(t + k, m)
        remote(lpart.at[pl.ds(pl.multiple_of(d * share, share), share)], lrecv.at[k - 1],
               l_send.at[k - 1], l_recv.at[k - 1], (f, d)).start()
    mine = pl.ds(pl.multiple_of(t * share, share), share)
    for k in range(1, m):
        remote(lpart.at[mine], lrecv.at[k - 1], l_send.at[k - 1], l_recv.at[k - 1], (f, t)).wait_recv()
    total = lpart[mine, :]
    for k in range(1, m):
        total = total + lrecv[k - 1]
    left_ref[mine, :] = total
    for k in range(1, m):
        d = lax.rem(t + k, m)
        remote(left_ref.at[mine], left_ref.at[mine], l2_send.at[k - 1], l2_recv.at[k - 1], (f, d)).start()
    for k in range(1, m):
        source = lax.rem(t - k + m, m)
        theirs = pl.ds(pl.multiple_of(source * share, share), share)
        remote(left_ref.at[theirs], left_ref.at[theirs], l2_send.at[k - 1], l2_recv.at[k - 1],
               (f, source)).wait_recv()

    left = left_ref[...]
    gpart[...] = dot(left, left, ((0,), (0,)))
    gshare = gpart.shape[0] // m
    gmine = pl.ds(pl.multiple_of(t * gshare, gshare), gshare)
    for k in range(1, n):
        d = lax.rem(f + k, n)
        remote(gpart.at[gmine], grecv.at[f], q_send.at[k - 1], q_recv.at[k - 1], (d, t)).start()
    grecv[f] = gpart[gmine, :]

    for j in range(wide // tile):
        col = slice(j * tile, (j + 1) * tile)
        spart[col, :] = dot(buf_ref[:, col], left, ((0,), (0,)))
    sshare = wide // n
    for k in range(1, n):
        d = lax.rem(f + k, n)
        remote(spart.at[pl.ds(pl.multiple_of(d * sshare, sshare), sshare)], srecv.at[k - 1],
               s_send.at[k - 1], s_recv.at[k - 1], (d, t)).start()

    for k in range(1, n):
        source = lax.rem(f - k + n, n)
        remote(gpart.at[gmine], grecv.at[source], q_send.at[k - 1], q_recv.at[k - 1],
               (source, t)).wait_recv()
    gram_ref[gmine, :] = jnp.sum(grecv[...], axis=0)
    for k in range(1, m):
        d = lax.rem(t + k, m)
        remote(gram_ref.at[gmine], gram_ref.at[gmine], q2_send.at[k - 1], q2_recv.at[k - 1],
               (f, d)).start()

    for k in range(1, m):
        source = lax.rem(t - k + m, m)
        theirs = pl.ds(pl.multiple_of(source * gshare, gshare), gshare)
        remote(gram_ref.at[theirs], gram_ref.at[theirs], q2_send.at[k - 1], q2_recv.at[k - 1],
               (f, source)).wait_recv()
    inv_ref[...] = jnp.zeros_like(inv_ref)
    inverse_begin(gram_ref, work)
    inverse_rows(work, inv_ref, 0, gram_ref.shape[0] // 2)
    smine = pl.ds(pl.multiple_of(f * sshare, sshare), sshare)
    for k in range(1, n):
        remote(spart.at[smine], srecv.at[k - 1], s_send.at[k - 1], s_recv.at[k - 1],
               (f, t)).wait_recv()
    total = spart[smine, :]
    for k in range(1, n):
        total = total + srecv[k - 1]
    s_ref[smine, :] = total

    def s_rows(owner):
        return s_ref.at[pl.ds(pl.multiple_of(owner * sshare, sshare), sshare)]

    def sz(owner, k):
        return remote(s_rows(owner), s_rows(owner), s2_send.at[k - 1], s2_recv.at[k - 1],
                      (lax.rem(z + k, nz) * 2 + x, t))

    def sx(owner, k):
        return remote(s_rows(owner), s_rows(owner), s2_send.at[nz - 1 + k], s2_recv.at[nz - 1 + k],
                      (xpeer, t))

    def owner_at(k, side):
        return lax.rem(z - k + nz, nz) * 2 + side

    for k in range(1, nz):
        sz(f, k).start()
    sx(f, 0).start()
    inverse_rows(work, inv_ref, gram_ref.shape[0] // 2, gram_ref.shape[0] * 3 // 4)
    for k in range(1, nz):
        sz(owner_at(k, x), k).wait_recv()
        sx(owner_at(k, x), k).start()

    inverse_rows(work, inv_ref, gram_ref.shape[0] * 3 // 4, gram_ref.shape[0])
    inv = inv_ref[...]
    for k in range(nz):
        sx(owner_at(k, 1 - x), k).wait_recv()
    right = dot(s_ref[...], inv, ((1,), (1,)))
    right_ref[...] = right
    squares[t] = jnp.broadcast_to(jnp.sum(right * right, axis=0, keepdims=True), squares.shape[1:])
    for k in range(1, m):
        remote(squares.at[t], squares.at[t], c_send.at[k - 1], c_recv.at[k - 1],
               (f, lax.rem(t + k, m))).start()
    basis_ref[...] = dot(left_ref[...], inv, ((1,), (1,)))
    for k in range(1, m):
        source = lax.rem(t - k + m, m)
        remote(squares.at[source], squares.at[source], c_send.at[k - 1], c_recv.at[k - 1],
               (f, source)).wait_recv()
    factor_ref[...] = lax.rsqrt(jnp.sum(squares[...], axis=0) / (rows * n) + 1e-06)

    store_buffer.wait()
    for k in range(1, n):
        d = lax.rem(f + k, n)
        remote(gsend.at[d], ggath.at[f, t], gs_send.at[k - 1], gs_recv.at[k - 1], (d, t)).wait_send()
        remote(gpart.at[gmine], grecv.at[f], q_send.at[k - 1], q_recv.at[k - 1], (d, t)).wait_send()
        remote(spart.at[pl.ds(pl.multiple_of(d * sshare, sshare), sshare)], srecv.at[k - 1],
               s_send.at[k - 1], s_recv.at[k - 1], (d, t)).wait_send()
    for k in range(1, m):
        d = lax.rem(t + k, m)
        remote(ggath.at[:, t], ggath.at[:, t], gt_send.at[k - 1], gt_recv.at[k - 1], (f, d)).wait_send()
        remote(lpart.at[pl.ds(pl.multiple_of(d * share, share), share)], lrecv.at[k - 1],
               l_send.at[k - 1], l_recv.at[k - 1], (f, d)).wait_send()
        remote(left_ref.at[mine], left_ref.at[mine], l2_send.at[k - 1], l2_recv.at[k - 1], (f, d)).wait_send()
        remote(gram_ref.at[gmine], gram_ref.at[gmine], q2_send.at[k - 1], q2_recv.at[k - 1],
               (f, d)).wait_send()
        remote(squares.at[t], squares.at[t], c_send.at[k - 1], c_recv.at[k - 1], (f, d)).wait_send()
    for k in range(nz):
        if k:
            sz(f, k).wait_send()
        sx(owner_at(k, x), k).wait_send()
    for zz in range(nz):
        for c in range(CHUNKS):
            ax(2 * zz + x, c).wait_send()
    for k in range(nz):
        for c in range(CHUNKS):
            pl.when((z >= k) & (z < nz - 1))(lambda k=k, c=c: az(f - 2 * k, c, 0, k).wait_send())
            pl.when((z + k < nz) & (z > 0))(lambda k=k, c=c: az(f + 2 * k, c, 1, k).wait_send())


def split3(v):
    h = v.astype(BF16)
    r = v - h.astype(F32)
    mid = r.astype(BF16)
    return h.astype(F32), mid.astype(F32), r - mid.astype(F32)


def inverse_begin(gram_ref, work):
    rank = gram_ref.shape[0]
    work[:, :rank] = gram_ref[...]
    row = lax.broadcasted_iota(jnp.int32, (rank, rank), 0)
    col = lax.broadcasted_iota(jnp.int32, (rank, rank), 1)
    work[:, rank:] = jnp.where(row == col, 1.0, 0.0).astype(F32)


def inverse_rows(work, inv_ref, first, last):
    rank = work.shape[0]
    some = LANES // 2
    sub = lax.broadcasted_iota(jnp.int32, (PANEL, 1), 0)
    for top in range(first, last, some):
        base = top // LANES * LANES
        end = rank + base + LANES
        lane = lax.broadcasted_iota(jnp.int32, (PANEL, rank - base), 1) + base

        def step(k, carry):
            start = pl.multiple_of(top + k * PANEL, PANEL)
            panel = work[pl.ds(start, PANEL), base:end]
            near = pltpu.roll(panel[:, :LANES], lax.rem(base + LANES - start, LANES), 1)
            pivots = jnp.ones((PANEL, 1), F32)
            for j in range(PANEL):
                column = near[:, j:j + 1]
                pivot = column[j:j + 1, :]
                weight = jnp.where(sub > j, column / pivot, 0.0)
                pivots = jnp.where(sub == j, pivot, pivots)
                near = near - weight * near[j:j + 1, :]
                panel = panel - weight * panel[j:j + 1, :]
            panel = panel * lax.rsqrt(pivots)
            inv_ref[pl.ds(start, PANEL), :base + LANES] = panel[:, rank - base:]
            outer = jnp.where(lane >= start + PANEL, panel[:, :rank - base], 0.0)[:, top - base:]
            h, mid, low = split3(outer)
            ph, pm, plow = split3(panel)
            lhs = jnp.concatenate([h, h, mid, h, mid, low], axis=0).astype(BF16)
            rhs = jnp.concatenate([ph, pm, ph, plow, pm, ph], axis=0).astype(BF16)
            work[top:, base:end] = work[top:, base:end] - lax.dot_general(
                lhs, rhs, (((0,), (0,)), ((), ())), preferred_element_type=F32)
            return carry

        lax.fori_loop(0, some // PANEL, step, 0)


def output_kernel(scale, buf_ref, basis_ref, right_ref, factor_ref, mom_ref, up_ref, hi, lo):
    @pl.when(pl.program_id(0) == 0)
    def _():
        r = right_ref[...]
        h = r.astype(BF16)
        hi[...] = h
        lo[...] = (r - h.astype(F32)).astype(BF16)

    basis = basis_ref[...]
    both = jnp.concatenate([basis * (momentum_decay - 1.0), basis * (factor_ref[0:1, :] * scale)], axis=0)
    bh = both.astype(BF16)
    bl = (both - bh.astype(F32)).astype(BF16)
    dims = (((1,), (1,)), ((), ()))
    out = lax.dot_general(bh, hi[...], dims, preferred_element_type=F32)
    out += lax.dot_general(bl, hi[...], dims, preferred_element_type=F32)
    out += lax.dot_general(bh, lo[...], dims, preferred_element_type=F32)
    tall = basis.shape[0]
    mom_ref[...] = buf_ref[...] + out[:tall]
    up_ref[...] = out[tall:]


def sds(*shape):
    return jax.ShapeDtypeStruct(shape, F32)


def kernels_on_device(n, m, activations, out_grad, momentum, right_prev):
    tok, wide = activations.shape
    rows = momentum.shape[0]
    rank = right_prev.shape[1]
    vm = pl.BlockSpec(memory_space=pltpu.VMEM)
    hbm = pl.BlockSpec(memory_space=pl.ANY)
    dma = pltpu.SemaphoreType.DMA
    nz = n // 2
    buffer, basis, right, factor = pl.pallas_call(
        functools.partial(main_kernel, n, m),
        out_shape=(sds(rows, wide), sds(rows, rank), sds(wide, rank), sds(8, rank)),
        in_specs=[vm, vm, hbm, hbm],
        out_specs=(hbm, vm, vm, vm),
        scratch_shapes=[
            pltpu.VMEM((rows, wide), F32),
            pltpu.VMEM((wide, rank), F32),
            dma((3,)),
            pltpu.VMEM((rows, rank), F32),
            pltpu.VMEM((rank, rank), F32),
            pltpu.VMEM((wide, rank), F32),
            pltpu.VMEM((rank, rank), F32),
            pltpu.VMEM((rank, 2 * rank), F32),
            pltpu.VMEM((m, 8, rank), F32),
            dma((m - 1,)), dma((m - 1,)),
            pltpu.VMEM((n, CHUNKS, tok // CHUNKS, wide), F32),
            pltpu.VMEM((n, m, tok // m, rows), F32),
            pltpu.VMEM((n, tok // m, rows), F32),
            pltpu.VMEM((rows, n * tok), BF16),
            pltpu.VMEM((rows, rank), F32),
            pltpu.VMEM((m - 1, rows // m, rank), F32),
            pltpu.VMEM((rank, rank), F32),
            pltpu.VMEM((n, rank // m, rank), F32),
            pltpu.VMEM((wide, rank), F32),
            pltpu.VMEM((n - 1, wide // n, rank), F32),
            dma((2, nz, CHUNKS)), dma((nz, CHUNKS)), dma((nz, CHUNKS)), dma((nz, CHUNKS)),
            dma((n - 1,)), dma((n - 1,)), dma((m - 1,)), dma((m - 1,)),
            dma((m - 1,)), dma((m - 1,)), dma((m - 1,)), dma((m - 1,)),
            dma((n - 1,)), dma((n - 1,)), dma((m - 1,)), dma((m - 1,)),
            dma((n - 1,)), dma((n - 1,)), dma((n - 1,)), dma((n - 1,)),
        ],
        compiler_params=pltpu.CompilerParams(
            collective_id=0, has_side_effects=True, vmem_limit_bytes=VMEM_LIMIT),
    )(activations, out_grad, momentum, right_prev)
    tall = LANES
    size = wide * m
    new_momentum, update = pl.pallas_call(
        functools.partial(output_kernel, math.sqrt(size / rank)),
        grid=(rows // tall,),
        out_shape=(sds(rows, wide), sds(rows, wide)),
        in_specs=[
            pl.BlockSpec((tall, wide), lambda i: (i, 0)),
            pl.BlockSpec((tall, rank), lambda i: (i, 0)),
            pl.BlockSpec((wide, rank), lambda i: (0, 0)),
            pl.BlockSpec((8, rank), lambda i: (0, 0)),
        ],
        out_specs=(
            pl.BlockSpec((tall, wide), lambda i: (i, 0)),
            pl.BlockSpec((tall, wide), lambda i: (i, 0)),
        ),
        scratch_shapes=[pltpu.VMEM((wide, rank), BF16)] * 2,
        compiler_params=pltpu.CompilerParams(vmem_limit_bytes=VMEM_LIMIT),
    )(buffer, basis, right, factor)
    own = rank // n
    first = lax.axis_index("fsdp") * own
    right_owned = lax.dynamic_slice_in_dim(right, first, own, 1) * lax.dynamic_slice_in_dim(
        factor[0:1], first, own, 1)
    return new_momentum, update, right_owned


def plain_on_device(activations, out_grad, momentum, right_prev):
    size = momentum.shape[1] * lax.axis_size("tp")
    rank = right_prev.shape[1]
    grad = lax.psum_scatter(
        lax.dot_general(out_grad, activations, (((0,), (0,)), ((), ())), preferred_element_type=F32),
        "fsdp", scatter_dimension=0, tiled=True)
    buffer = momentum + grad
    left = lax.psum(dot(buffer, right_prev), "tp")
    gram = lax.psum(dot(left.T, left), "fsdp")
    lower = jnp.linalg.cholesky(gram)
    basis = lax.linalg.triangular_solve(lower, left, left_side=False, lower=True, transpose_a=True)
    right = lax.psum(dot(buffer.T, basis), "fsdp")
    squares = lax.psum(jnp.sum(right * right, axis=0), "tp")
    factor = lax.rsqrt(squares / size + 1e-06)
    right_next = right * factor[None, :]
    new_momentum = buffer - (1.0 - momentum_decay) * dot(basis, right.T)
    update = math.sqrt(size / rank) * dot(basis, right_next.T)
    own = rank // lax.axis_size("fsdp")
    right_owned = lax.dynamic_slice_in_dim(right_next, lax.axis_index("fsdp") * own, own, 1)
    return new_momentum, update, right_owned


def solution(mesh):
    n, m = mesh.shape["fsdp"], mesh.shape["tp"]

    def on_device(activations, out_grad, momentum, right_prev):
        tok, wide = activations.shape
        rows = momentum.shape[0]
        if rows % LANES == 0 and wide % (2 * LANES) == 0 and 4 * n * tok * (wide + rows) <= VMEM_LIMIT // 4:
            return kernels_on_device(n, m, activations, out_grad, momentum, right_prev)
        return plain_on_device(activations, out_grad, momentum, right_prev)

    return jax.shard_map(
        on_device,
        mesh=mesh,
        in_specs=(P("fsdp", "tp"), P("fsdp", None), P("fsdp", "tp"), P("tp", None)),
        out_specs=(P("fsdp", "tp"), P("fsdp", "tp"), P("tp", "fsdp")),
        check_vma=False,
    )
```
